512 devices in a mesh: dp: 32 (over z, core), tensor: 16 (over x, y).
Axes of the slice: x: 4, y: 4, z: 16, core: 2. Of those that a mesh axis runs over, the one named last changes fastest.
Arguments:
- hidden_in: bfloat16 [16384, 8192], P('dp', 'tensor'), may hold values from -6 to 6
- norm_gain: float32 [8192], P('tensor'), may hold values from 0.5 to 1.5
- key_weight: bfloat16 [8192, 512], P('tensor'), as said below
- value_weight: bfloat16 [8192, 512], P('tensor'), may hold values from -0.0625 to 0.0625
- queries: bfloat16 [16384, 4096], P('dp', 'tensor'), may hold values from -8 to 8
- segments: int32 [32, 512], P('dp'), may hold values from 0 to 3, never falling along the last dimension, each value on 1 to 256 neighbouring positions
- cotangent: bfloat16 [16384, 4096], P('dp', 'tensor'), may hold values from -6 to 6
Outputs:
- attn_out: bfloat16 [16384, 4096], P('dp', 'tensor')
- grad_hidden: bfloat16 [16384, 8192], P('dp', 'tensor')
- grad_queries: bfloat16 [16384, 4096], P('dp', 'tensor')
- grad_key_weight: float32 [8192, 512], P(('tensor', 'dp'))
- grad_value_weight: float32 [8192, 512], P(('tensor', 'dp'))
- grad_gain: float32 [8192], P(('tensor', 'dp'))
The draws below stay inside these ranges and needn't reach their ends.
Inputs may be any that keep to these rules, and one draw needn't show every extreme that they name: `segments`: segment numbers never fall along a row; each document has 1 to 256 tokens, one exactly 256. `key_weight`: entries have a standard deviation of about 8192^(-1/2) and lie within 6 such deviations.
All inputs are finite; a program needn't handle non-finite values.
Results may differ from the reference program's by a relative error of at most 0.035.
Values may be sent and summed in bfloat16 or wider, within the bound.
No kernel may reach another device: no remote copies, remote signals or barrier semaphores. Data moves between devices by JAX's collectives and lax.ppermute only.
A program may use at most 64 MiB of HBM per device.

```python
import math
import jax
import jax.numpy as jnp
import numpy as np
from jax import lax

D = 8192
HQ = 32
KVH = 4
HD = 128
SEQ = 512
TOKENS = 16384
N_DP = 32


def column_scales(factor):
    place = jnp.arange(D).astype(jnp.float32) / D
    return 1.5 * jnp.exp(jnp.log(factor) * (place - 1.0))


def draw_key_weight(key, part):
    key = jax.random.fold_in(key, 7)
    noise = jax.random.normal(key, (D, KVH, HD), jnp.float32)
    weight = jnp.clip(noise, -6.0, 6.0)
    return (weight * D ** (-0.5)).reshape(D, KVH * HD).astype(jnp.bfloat16)


def draw_hidden_in(key, part):
    key = jax.random.fold_in(key, 13)
    key_base = jax.random.fold_in(key, 0)
    values = jax.random.normal(key_base, (TOKENS, D), jnp.float32)
    values = jnp.clip(values * column_scales(4.0)[None, :], -6.0, 6.0)
    return values.astype(jnp.bfloat16)


def draw_queries(key, part):
    key = jax.random.fold_in(key, 17)
    key_base = jax.random.fold_in(key, 0)
    values = jnp.clip(jax.random.normal(key_base, (TOKENS, HQ * HD), jnp.float32), -6.0, 6.0)
    return values.astype(jnp.bfloat16)


def block_scale(own_key, dims, cuts, smallest, high):
    factor_of, own = 1.0, jax.random.fold_in(own_key, 6)
    for axis_at, shards_of in cuts:
        draws = jnp.exp(jax.random.uniform(jax.random.fold_in(own, axis_at), (shards_of,), jnp.float32, smallest / len(cuts), high / len(cuts)))
        factor_of = factor_of * jnp.repeat(draws, dims[axis_at] // shards_of).reshape([-1 if axis == axis_at else 1 for axis in range(len(dims))])
    return factor_of


def length_profile(count, total, bound, lean):
    weights = [(1 << 20) // math.isqrt(rank ** lean) + 1 for rank in range(2, count + 1)]
    spare, holding = total - bound - (count - 1), [1] * (count - 1)
    while spare > 0:
        candidates = [i for i in range(count - 1) if holding[i] < bound]
        whole, budget = sum([weights[i] for i in candidates]), spare
        for i in candidates:
            more = min(bound - holding[i], max(1, budget * weights[i] // whole), spare)
            holding[i] = holding[i] + more
            spare = spare - more
    return np.array([bound] + holding)


def ragged(rng, count, total, most, slope):
    if count == 2:
        one = jax.random.randint(rng, (), max(1, total - most), min(most, total - 1) + 1)
        return jnp.stack([one, total - one])
    lengths = jnp.asarray(length_profile(count, total, most, slope), jnp.int32)
    pairs = (count - 1) // 2
    donor, sink = lengths[1:1 + 2 * pairs:2], lengths[2:2 + 2 * pairs:2]
    slack = jnp.minimum(donor - 1, most - sink)
    moved = jax.random.randint(jax.random.fold_in(rng, 1), (pairs,), 0, 1 << 20) % (slack + 1)
    lengths = lengths.at[1:1 + 2 * pairs:2].set(donor - moved).at[2:2 + 2 * pairs:2].set(sink + moved)
    return lengths[jax.random.permutation(jax.random.fold_in(rng, 2), count)]


def centred(own_key, shape, deviation, limit, shards=(), kind=jnp.bfloat16):
    array = jax.random.normal(own_key, shape, jnp.float32) * deviation
    if len(shards) > 0:
        array = block_scale(own_key, shape, shards, -0.22, 0.18) * array
    return jnp.clip(array, min=-limit, max=limit).astype(kind)


def setup_inputs(seed: int = 0) -> dict:
    streams_of = jax.random.split(jax.random.key(seed), 8)
    hidden_in = draw_hidden_in(jax.random.fold_in(streams_of[7], 71), 0)
    norm_gain = jnp.clip(1.0 + 0.1 * jax.random.normal(streams_of[1], (D,), jnp.float32), 0.5, 1.5)
    key_weight = draw_key_weight(jax.random.fold_in(streams_of[7], 71), 0)
    value_weight = centred(streams_of[3], (D, KVH * HD), D ** -0.5, 0.0625, ((0, 16),))
    queries = draw_queries(jax.random.fold_in(streams_of[7], 71), 0)
    segments = jax.vmap(lambda own: jnp.searchsorted(jnp.cumsum(ragged(own, 4, SEQ, SEQ // 2, 0)), jnp.arange(SEQ), side="right"))(jax.random.split(streams_of[5], N_DP)).reshape((N_DP, SEQ)).astype(jnp.int32)
    cotangent = centred(streams_of[6], (TOKENS, HQ * HD), 1.0, 6.0, ((0, 32), (1, 16)))
    return {"hidden_in": hidden_in, "norm_gain": norm_gain, "key_weight": key_weight, "value_weight": value_weight, "queries": queries, "segments": segments, "cotangent": cotangent}


ROPE_BASE = 500000.0

def angles(pos, head_size, ndim):
    half = head_size // 2
    freq = ROPE_BASE ** (-(jnp.arange(half).astype(jnp.float32) * 2.0 / head_size))
    angle = pos[:, None] * freq[None, :]
    shape = (pos.shape[0],) + (1,) * (ndim - 2) + (half,)
    return (jnp.cos(angle).reshape(shape), jnp.sin(angle).reshape(shape))

def rotate(vec, pos, sign):
    half = vec.shape[-1] // 2
    cosine, sine = angles(pos, vec.shape[-1], vec.ndim)
    first = vec[..., :half]
    second = vec[..., half:]
    return jnp.concatenate([first * cosine - sign * second * sine, second * cosine + sign * first * sine], axis=-1)

def row_layout(seg):
    rows = seg.shape[0]
    index = jnp.arange(rows).astype(jnp.int32)
    same = seg[:, None] == seg[None, :]
    start = lax.optimization_barrier(jnp.min(jnp.where(same, index[None, :], rows), axis=1))
    pos = (index - start).astype(jnp.float32)
    allowed = same & (index[None, :] <= index[:, None])
    return (pos, allowed)

def one_row(hidden_in, norm_gain, key_weight, value_weight, queries, seg, cotangent):
    rows = hidden_in.shape[0]
    group = HQ // KVH
    scale = 1.0 / HD ** 0.5
    in_float = hidden_in.astype(jnp.float32)
    inv_rms = lax.rsqrt(lax.optimization_barrier(jnp.sum(in_float * in_float, axis=1)) / D + 1e-05)
    unit = in_float * inv_rms[:, None]
    normed = (unit * norm_gain[None, :]).astype(jnp.bfloat16)
    keys = jnp.dot(normed, key_weight, preferred_element_type=jnp.float32).astype(jnp.bfloat16)
    values = jnp.dot(normed, value_weight, preferred_element_type=jnp.float32).astype(jnp.bfloat16)
    pos, allowed = row_layout(seg)
    query_four = queries.astype(jnp.float32).reshape(rows, KVH, group, HD)
    q_rot = rotate(query_four, pos, 1.0).astype(jnp.bfloat16).astype(jnp.float32)
    k_rot = rotate(keys.astype(jnp.float32).reshape(rows, KVH, HD), pos, 1.0).astype(jnp.bfloat16).astype(jnp.float32)
    val_three = values.astype(jnp.float32).reshape(rows, KVH, HD)
    scores = jnp.einsum('qcrd,kcd->crqk', q_rot, k_rot) * scale
    scores = jnp.where(allowed[None, None], scores, -1e+30)
    top = lax.optimization_barrier(jnp.max(scores, axis=-1, keepdims=True))
    expo = jnp.exp(scores - top)
    probs = (expo / lax.optimization_barrier(jnp.sum(expo, axis=-1, keepdims=True))).astype(jnp.bfloat16).astype(jnp.float32)
    attn_out = jnp.einsum('crqk,kcd->qcrd', probs, val_three).astype(jnp.bfloat16).reshape(rows, HQ * HD)
    cot_four = cotangent.astype(jnp.float32).reshape(rows, KVH, group, HD)
    d_probs = jnp.einsum('qcrd,kcd->crqk', cot_four, val_three)
    delta = lax.optimization_barrier(jnp.sum(probs * d_probs, axis=-1, keepdims=True))
    d_scores = (probs * (d_probs - delta) * scale).astype(jnp.bfloat16).astype(jnp.float32)
    d_qrot = jnp.einsum('crqk,kcd->qcrd', d_scores, k_rot)
    grad_queries = rotate(d_qrot, pos, -1.0).astype(jnp.bfloat16).reshape(rows, HQ * HD)
    d_krot = jnp.einsum('crqk,qcrd->kcd', d_scores, q_rot)
    d_keys = rotate(d_krot, pos, -1.0).astype(jnp.bfloat16).reshape(rows, KVH * HD)
    d_values = jnp.einsum('crqk,qcrd->kcd', probs, cot_four).astype(jnp.bfloat16).reshape(rows, KVH * HD)
    d_normed = jnp.dot(d_keys, key_weight.T, preferred_element_type=jnp.float32) + jnp.dot(d_values, value_weight.T, preferred_element_type=jnp.float32)
    grad_key = jnp.dot(normed.T, d_keys, preferred_element_type=jnp.float32)
    grad_value = jnp.dot(normed.T, d_values, preferred_element_type=jnp.float32)
    grad_gain = lax.optimization_barrier(jnp.sum(d_normed * unit, axis=0))
    d_unit = d_normed * norm_gain[None, :]
    corr = lax.optimization_barrier(jnp.sum(d_unit * unit, axis=1)) / D
    grad_hidden = (inv_rms[:, None] * (d_unit - unit * corr[:, None])).astype(jnp.bfloat16)
    return (attn_out, grad_hidden, grad_queries, grad_key, grad_value, grad_gain)

def reference(hidden_in, norm_gain, key_weight, value_weight, queries, segments, cotangent):
    nrows = segments.shape[0]
    hidden_rows = hidden_in.reshape(nrows, SEQ, D)
    query_rows = queries.reshape(nrows, SEQ, HQ * HD)
    cot_rows = cotangent.reshape(nrows, SEQ, HQ * HD)

    def step(carry, item):
        hid, qry, seg, cot = item
        attn_out, grad_hidden, grad_queries, grad_key, grad_value, grad_gain = one_row(hid, norm_gain, key_weight, value_weight, qry, seg, cot)
        carry = (carry[0] + grad_key, carry[1] + grad_value, carry[2] + grad_gain)
        return (carry, (attn_out, grad_hidden, grad_queries))
    start = (jnp.zeros((D, KVH * HD), jnp.float32), jnp.zeros((D, KVH * HD), jnp.float32), jnp.zeros((D,), jnp.float32))
    sums, outs = lax.scan(step, start, (hidden_rows, query_rows, segments, cot_rows))
    attn_out = outs[0].reshape(nrows * SEQ, HQ * HD)
    grad_hidden = outs[1].reshape(nrows * SEQ, D)
    grad_queries = outs[2].reshape(nrows * SEQ, HQ * HD)
    return (attn_out, grad_hidden, grad_queries, sums[0], sums[1], sums[2])
```

```python
import functools

import jax
import jax.numpy as jnp
import numpy as np
from jax import lax
from jax.experimental import pallas as pl
from jax.experimental.pallas import tpu as pltpu
from jax.sharding import Mesh, PartitionSpec as P

D = 8192
SEQ = 512
KVH = 4
HD = 128
SCALE = 1.0 / HD**0.5
ROPE_BASE = 500000.0
Q = 128
CH = Q + 16
NT = (((1,), (1,)), ((), ()))
TN = (((0,), (0,)), ((), ()))
BF = jnp.bfloat16
F32 = jnp.float32


def rope_tables():
    half = HD // 2
    freq = np.float32(ROPE_BASE) ** (-(np.arange(half, dtype=np.float32) * np.float32(2.0 / HD)))
    angle = (np.arange(SEQ, dtype=np.float32)[:, None] * freq[None, :]).astype(np.float64)
    cos, sin = np.cos(angle), np.sin(angle)
    return (
        np.concatenate([cos, cos], axis=1).astype(np.float32),
        np.concatenate([-sin, sin], axis=1).astype(np.float32),
    )


def eye(n):
    return lax.broadcasted_iota(jnp.int32, (n, n), 0) == lax.broadcasted_iota(jnp.int32, (n, n), 1)


def to_column(row, diag):
    return jnp.sum(jnp.where(diag, row, 0.0), axis=1, keepdims=True)


def to_row(column, diag):
    return jnp.sum(jnp.where(diag, column, 0.0), axis=0, keepdims=True)


def two_halves(row):
    lead = row.astype(BF)
    rest = (row - lead.astype(F32)).astype(BF)
    return jnp.broadcast_to(jnp.concatenate([lead, rest], axis=1), (16, 2 * HD))


def from_halves(tile):
    both = tile.astype(F32)
    return both[0:1, :HD] + both[0:1, HD:]


def turn(vec, cos, sin):
    return vec * cos + pltpu.roll(vec, HD // 2, 1) * sin


def turn_back(vec, cos, sin):
    return vec * cos - pltpu.roll(vec, HD // 2, 1) * sin


def project_kernel(hid_ref, gain_ref, wk_ref, wv_ref, out_ref):
    wk = wk_ref[...]
    wv = wv_ref[...]
    ones = jnp.ones((16, hid_ref.shape[1]), BF)
    for quarter in range(SEQ // Q):
        hid = hid_ref[quarter * Q : (quarter + 1) * Q, :].astype(F32)
        scaled = (hid * gain_ref[...]).astype(BF)
        part_k = jnp.dot(scaled, wk, preferred_element_type=F32).astype(BF)
        part_v = jnp.dot(scaled, wv, preferred_element_type=F32).astype(BF)
        square = hid * hid
        lead = square.astype(BF)
        rest = (square - lead.astype(F32)).astype(BF)
        sums = lax.dot_general(ones, lead, NT, preferred_element_type=F32)
        sums += lax.dot_general(ones, rest, NT, preferred_element_type=F32)
        tile = two_halves(sums[0:1, :])
        for head in range(KVH):
            at = head * (SEQ // Q) + quarter
            cols = slice(head * HD, (head + 1) * HD)
            out_ref[at, 0:Q, 0:HD] = part_k[:, cols]
            out_ref[at, 0:Q, HD:] = part_v[:, cols]
            out_ref[at, Q:CH, :] = tile


def combine_kernel(place_ref, got_ref, cos_ref, sin_ref, out_ref):
    total = got_ref[0].astype(F32)
    for at in range(1, got_ref.shape[0]):
        total += got_ref[at].astype(F32)
    square = total[Q : Q + 1, :HD] + total[Q : Q + 1, HD:]
    inv_row = lax.rsqrt(square / D + 1e-05)
    inv = to_column(inv_row, eye(Q))
    first = pl.multiple_of(place_ref[0] * Q, Q)
    keys = (total[:Q, :HD] * inv).astype(BF).astype(F32)
    keys = turn(keys, cos_ref[pl.ds(first, Q), :], sin_ref[pl.ds(first, Q), :]).astype(BF)
    values = (total[:Q, HD:] * inv).astype(BF)
    tile = two_halves(inv_row)
    for at in range(out_ref.shape[0]):
        out_ref[at, 0:Q, 0:HD] = keys
        out_ref[at, 0:Q, HD:] = values
        out_ref[at, Q:CH, :] = tile


def attention_kernel(
    kv_ref, q_ref, cot_ref, seg_ref, cos_ref, sin_ref, out_ref, gq_ref, gkv_ref, dk_ref, dv_ref
):
    blocks = SEQ // Q
    diag = eye(Q)
    seg_rows = [seg_ref[0:1, b * Q : (b + 1) * Q].astype(F32) for b in range(blocks)]
    seg_columns = [to_column(row, diag) for row in seg_rows]
    below = lax.broadcasted_iota(jnp.int32, (Q, Q), 0) <= lax.broadcasted_iota(
        jnp.int32, (Q, Q), 1
    )
    dk_ref[...] = jnp.zeros_like(dk_ref)
    dv_ref[...] = jnp.zeros_like(dv_ref)
    for b in range(blocks):
        rows = slice(b * Q, (b + 1) * Q)
        low = max(0, b - 2)
        keys = jnp.concatenate([kv_ref[a, 0:Q, 0:HD] for a in range(low, b + 1)], axis=0)
        values = jnp.concatenate([kv_ref[a, 0:Q, HD:] for a in range(low, b + 1)], axis=0)
        cos, sin = cos_ref[rows, :], sin_ref[rows, :]
        q_rot = jnp.concatenate(
            [
                turn(q_ref[rows, h * HD : (h + 1) * HD].astype(F32), cos, sin).astype(BF)
                for h in range(2)
            ],
            axis=0,
        )
        cot = jnp.concatenate([cot_ref[rows, 0:HD], cot_ref[rows, HD:]], axis=0)
        allowed = [seg_columns[a] == seg_rows[b] for a in range(low, b)]
        allowed.append((seg_columns[b] == seg_rows[b]) & below)
        allowed = jnp.concatenate([jnp.where(a, 0.0, -1e30) for a in allowed], axis=0)
        allowed = jnp.concatenate([allowed, allowed], axis=1)
        scores = lax.dot_general(keys, q_rot, NT, preferred_element_type=F32) * SCALE
        scores = jnp.where(allowed < 0.0, -1e30, scores)
        top = jnp.max(scores, axis=0, keepdims=True)
        expo = jnp.exp(scores - top)
        probs = (expo * (1.0 / jnp.sum(expo, axis=0, keepdims=True))).astype(BF)
        d_probs = lax.dot_general(values, cot, NT, preferred_element_type=F32)
        prob_float = probs.astype(F32)
        delta = jnp.sum(prob_float * d_probs, axis=0, keepdims=True)
        d_scores = (prob_float * (d_probs - delta) * SCALE).astype(BF)
        attn = lax.dot_general(probs, values, TN, preferred_element_type=F32)
        d_q = lax.dot_general(d_scores, keys, TN, preferred_element_type=F32)
        for h in range(2):
            cols = slice(h * HD, (h + 1) * HD)
            out_ref[rows, cols] = attn[h * Q : (h + 1) * Q].astype(BF)
            gq_ref[rows, cols] = turn_back(d_q[h * Q : (h + 1) * Q], cos, sin).astype(BF)
        span = slice(low * Q, (b + 1) * Q)
        dv_ref[span, :] += jnp.dot(probs, cot, preferred_element_type=F32)
        dk_ref[span, :] += jnp.dot(d_scores, q_rot, preferred_element_type=F32)
    for b in range(blocks):
        rows = slice(b * Q, (b + 1) * Q)
        gkv_ref[b, :, 0:HD] = dk_ref[rows, :].astype(BF)
        gkv_ref[b, :, HD:] = dv_ref[rows, :].astype(BF)


def grad_sum_kernel(place_ref, got_ref, kv_ref, cos_ref, sin_ref, out_ref):
    total = got_ref[0].astype(F32)
    for at in range(1, got_ref.shape[0]):
        total += got_ref[at].astype(F32)
    own = kv_ref[0, 0:Q, :].astype(F32)
    corr = to_row(jnp.sum(total * own, axis=1, keepdims=True), eye(Q))
    first = pl.multiple_of(place_ref[0] * Q, Q)
    d_keys = turn_back(total[:, :HD], cos_ref[pl.ds(first, Q), :], sin_ref[pl.ds(first, Q), :])
    both = jnp.concatenate([d_keys, total[:, HD:]], axis=1).astype(BF)
    tile = two_halves(corr)
    for at in range(out_ref.shape[0]):
        out_ref[at, 0:Q, :] = both
        out_ref[at, Q:CH, :] = tile


def weight_kernel(place_ref, got_ref, kv_ref, hid_ref, send_ref, keep_ref, scaled_ref, raw_ref):
    blocks = SEQ // Q
    width = KVH * HD
    diag = eye(Q)
    for b in range(blocks):
        inv = to_column(from_halves(kv_ref[b, Q:CH, :]), diag)
        for head in range(KVH):
            part = (got_ref[head * blocks + b, 0:Q, :].astype(F32) * inv).astype(BF)
            cols = slice(head * HD, (head + 1) * HD)
            scaled_ref[b * Q : (b + 1) * Q, cols] = part[:, :HD]
            scaled_ref[b * Q : (b + 1) * Q, width + head * HD : width + (head + 1) * HD] = part[
                :, HD:
            ]
    scaled = scaled_ref[...]
    for f in range(hid_ref.shape[1] // HD):
        cols = slice(f * HD, (f + 1) * HD)
        raw_ref[cols, :] = lax.dot_general(
            hid_ref[:, cols], scaled, TN, preferred_element_type=F32
        ).astype(BF)
    core = place_ref[1]
    count, step = send_ref.shape[0], send_ref.shape[1]
    for at in range(count):
        mine = pl.multiple_of((2 * at + core) * step, step)
        other = pl.multiple_of((2 * at + 1 - core) * step, step)
        keep_ref[at] = raw_ref[pl.ds(mine, step), :]
        send_ref[at] = raw_ref[pl.ds(other, step), :]


def hidden_kernel(got_ref, kv_ref, hid_ref, gain_ref, wk_ref, wv_ref, out_ref):
    blocks = SEQ // Q
    diag = eye(Q)
    wk, wv = wk_ref[...], wv_ref[...]
    for b in range(blocks):
        rows = slice(b * Q, (b + 1) * Q)
        mine = [got_ref[head * blocks + b] for head in range(KVH)]
        d_keys = jnp.concatenate([m[0:Q, :HD] for m in mine], axis=1)
        d_values = jnp.concatenate([m[0:Q, HD:] for m in mine], axis=1)
        inv = to_column(from_halves(kv_ref[b, Q:CH, :]), diag)
        corr = sum(from_halves(m[Q:CH, :]) for m in mine)
        corr = to_column(corr, diag) / D
        d_normed = lax.dot_general(d_keys, wk, NT, preferred_element_type=F32)
        d_normed += lax.dot_general(d_values, wv, NT, preferred_element_type=F32)
        unit = hid_ref[rows, :].astype(F32) * inv
        out_ref[rows, :] = (inv * (d_normed * gain_ref[...] - unit * corr)).astype(BF)


def pair_kernel(keep_ref, got_ref, out_ref):
    out_ref[...] = (keep_ref[...].astype(F32) + got_ref[...].astype(F32)).astype(BF)


def finish_kernel(place_ref, got_ref, gain_ref, wk_ref, wv_ref, gk_ref, gv_ref, gg_ref):
    step = got_ref.shape[1]
    width = KVH * HD
    total = got_ref[0].astype(F32)
    for at in range(1, got_ref.shape[0]):
        total += got_ref[at].astype(F32)
    first = pl.multiple_of(place_ref[2] * step, step)
    lanes = lax.broadcasted_iota(jnp.int32, (step, gain_ref.shape[1]), 1)
    rows = lax.broadcasted_iota(jnp.int32, (step, gain_ref.shape[1]), 0)
    gain = jnp.sum(jnp.where(lanes == rows + first, gain_ref[...], 0.0), axis=1, keepdims=True)
    gk_ref[...] = total[:, :width] * gain
    gv_ref[...] = total[:, width:] * gain
    along = wk_ref[pl.ds(first, step), :].astype(F32) * total[:, :width]
    along += wv_ref[pl.ds(first, step), :].astype(F32) * total[:, width:]
    gg_ref[...] = to_row(jnp.sum(along, axis=1, keepdims=True), eye(step))


def call(kernel, out_shape, smem=0, args=0, scratch=(), name=None):
    specs = [pl.BlockSpec(memory_space=pltpu.SMEM)] * smem
    specs += [pl.BlockSpec(memory_space=pltpu.VMEM)] * args
    vmem = pl.BlockSpec(memory_space=pltpu.VMEM)
    out_specs = [vmem] * len(out_shape) if isinstance(out_shape, (list, tuple)) else vmem
    return pl.pallas_call(
        kernel,
        out_shape=out_shape,
        in_specs=specs,
        out_specs=out_specs,
        scratch_shapes=list(scratch),
        compiler_params=pltpu.CompilerParams(vmem_limit_bytes=40 * 1024 * 1024),
        name=name,
    )


def body(nz, hidden_in, norm_gain, key_weight, value_weight, queries, segments, cotangent):
    shape = jax.ShapeDtypeStruct
    width = KVH * HD
    feats = hidden_in.shape[1]
    step = feats // (2 * nz)
    cos, sin = (jnp.asarray(t) for t in rope_tables())
    gain = norm_gain.reshape(1, feats)
    core = lax.axis_index("core")
    place = jnp.stack([lax.axis_index("y"), core, lax.axis_index("z") * 2 + core]).astype(jnp.int32)

    parts = call(project_kernel, shape((16, CH, 2 * HD), BF), 0, 4, name="project")(
        hidden_in, gain, key_weight, value_weight
    )
    parts = lax.all_to_all(parts, ("x", "y"), 0, 0, tiled=True)
    own = call(combine_kernel, shape((4, CH, 2 * HD), BF), 1, 3, name="combine")(
        place, parts, cos, sin
    )
    kv = lax.all_to_all(own, "y", 0, 0, tiled=True)
    attn_out, grad_queries, grad_parts = call(
        attention_kernel,
        [shape(queries.shape, BF), shape(queries.shape, BF), shape((4, Q, 2 * HD), BF)],
        0,
        6,
        [pltpu.VMEM((SEQ, HD), F32), pltpu.VMEM((SEQ, HD), F32)],
        name="attention",
    )(kv, queries, cotangent, segments, cos, sin)
    grad_parts = lax.all_to_all(grad_parts, "y", 0, 0, tiled=True)
    grad_own = call(grad_sum_kernel, shape((16, CH, 2 * HD), BF), 1, 4, name="grad_sum")(
        place, grad_parts, own, cos, sin
    )
    grads = lax.all_to_all(grad_own, ("x", "y"), 0, 0, tiled=True)
    send, keep = call(
        weight_kernel,
        [shape((nz, step, 2 * width), BF), shape((nz, step, 2 * width), BF)],
        1,
        3,
        [pltpu.VMEM((SEQ, 2 * width), BF), pltpu.VMEM((feats, 2 * width), BF)],
        name="weight",
    )(place, grads, kv, hidden_in)
    got = lax.ppermute(send, "core", [(0, 1), (1, 0)])
    grad_hidden = call(hidden_kernel, shape(hidden_in.shape, BF), 0, 6, name="hidden")(
        grads, kv, hidden_in, gain, key_weight, value_weight
    )
    pair = call(pair_kernel, shape(keep.shape, BF), 0, 2, name="pair")(keep, got)
    rows = lax.all_to_all(pair, "z", 0, 0, tiled=True)
    grad_key, grad_value, grad_gain = call(
        finish_kernel,
        [shape((step, width), F32), shape((step, width), F32), shape((1, step), F32)],
        1,
        4,
        name="finish",
    )(place, rows, gain, key_weight, value_weight)
    return (attn_out, grad_hidden, grad_queries, grad_key, grad_value, grad_gain.reshape(step))


def solution(mesh):
    nz = mesh.devices.shape[0] // 2
    split = Mesh(mesh.devices.reshape(nz, 2, 4, 4), ("z", "core", "x", "y"))
    dp, tensor = ("z", "core"), ("x", "y")
    return jax.shard_map(
        functools.partial(body, nz),
        mesh=split,
        in_specs=(
            P(dp, tensor),
            P(tensor),
            P(tensor, None),
            P(tensor, None),
            P(dp, tensor),
            P(dp, None),
            P(dp, tensor),
        ),
        out_specs=(
            P(dp, tensor),
            P(dp, tensor),
            P(dp, tensor),
            P(tensor + dp, None),
            P(tensor + dp, None),
            P(tensor + dp),
        ),
        check_vma=False,
    )
```

```python
import functools

import jax
import jax.numpy as jnp
import numpy as np
from jax import lax
from jax.experimental import pallas as pl
from jax.experimental.pallas import tpu as pltpu
from jax.sharding import Mesh, PartitionSpec as P

D = 8192
SEQ = 512
KVH = 4
HD = 128
SCALE = 1.0 / HD**0.5
ROPE_BASE = 500000.0
Q = 128
CH = 2 * Q + 16
NT = (((1,), (1,)), ((), ()))
TN = (((0,), (0,)), ((), ()))
BF = jnp.bfloat16
F32 = jnp.float32


def rope_tables():
    half = HD // 2
    freq = np.float32(ROPE_BASE) ** (-(np.arange(half, dtype=np.float32) * np.float32(2.0 / HD)))
    angle = (np.arange(SEQ, dtype=np.float32)[:, None] * freq[None, :]).astype(np.float64)
    cos, sin = np.cos(angle), np.sin(angle)
    return (
        np.concatenate([cos, cos], axis=1).astype(np.float32),
        np.concatenate([-sin, sin], axis=1).astype(np.float32),
    )


def eye(n):
    return lax.broadcasted_iota(jnp.int32, (n, n), 0) == lax.broadcasted_iota(jnp.int32, (n, n), 1)


def to_column(row, diag):
    return jnp.sum(jnp.where(diag, row, 0.0), axis=1, keepdims=True)


def to_row(column, diag):
    return jnp.sum(jnp.where(diag, column, 0.0), axis=0, keepdims=True)


def two_halves(row):
    lead = row.astype(BF)
    rest = (row - lead.astype(F32)).astype(BF)
    at = lax.broadcasted_iota(jnp.int32, (16, HD), 0)
    zero = jnp.zeros((), F32)
    both = jnp.where(at == 0, lead.astype(F32), jnp.where(at == 1, rest.astype(F32), zero))
    return both.astype(BF)


def from_halves(tile):
    both = tile.astype(F32)
    return both[0:1, :] + both[1:2, :]


def turn(vec, cos, sin):
    return vec * cos + pltpu.roll(vec, HD // 2, 1) * sin


def turn_back(vec, cos, sin):
    return vec * cos - pltpu.roll(vec, HD // 2, 1) * sin


def total_of(got_ref):
    total = got_ref[0].astype(F32)
    for at in range(1, got_ref.shape[0]):
        total += got_ref[at].astype(F32)
    return total


def project_kernel(
    hid_hbm, gain_hbm, wk_hbm, wv_hbm, out_hbm, hid_ref, gain_ref, wk_ref, wv_ref, out_ref, sem, out_sem
):
    quarters = SEQ // Q
    feats = hid_ref.shape[1]
    copies = [pltpu.make_async_copy(gain_hbm, gain_ref, sem.at[0])]
    for at in range(quarters):
        rows = pl.ds(at * Q, Q)
        copies.append(pltpu.make_async_copy(hid_hbm.at[rows, :], hid_ref.at[rows, :], sem.at[1 + at]))
    part = feats // 4
    for which, (src, dst) in enumerate(((wk_hbm, wk_ref), (wv_hbm, wv_ref))):
        for at in range(4):
            rows = pl.ds(at * part, part)
            copies.append(
                pltpu.make_async_copy(src.at[rows, :], dst.at[rows, :], sem.at[5 + 4 * which + at])
            )
    for copy in copies:
        copy.start()
    ones = jnp.ones((16, feats), BF)
    sent = []
    for quarter in range(quarters):
        if quarter == 0:
            copies[0].wait()
        copies[1 + quarter].wait()
        hid = hid_ref[quarter * Q : (quarter + 1) * Q, :].astype(F32)
        scaled = (hid * gain_ref[...]).astype(BF)
        square = hid * hid
        lead = square.astype(BF)
        rest = (square - lead.astype(F32)).astype(BF)
        sums = lax.dot_general(ones, lead, NT, preferred_element_type=F32)
        sums += lax.dot_general(ones, rest, NT, preferred_element_type=F32)
        tile = two_halves(sums[0:1, :])
        if quarter == 0:
            for copy in copies[5:9]:
                copy.wait()
        part_k = jnp.dot(scaled, wk_ref[...], preferred_element_type=F32).astype(BF)
        if quarter == 0:
            for copy in copies[9:13]:
                copy.wait()
        part_v = jnp.dot(scaled, wv_ref[...], preferred_element_type=F32).astype(BF)
        for head in range(KVH):
            at = head * quarters + quarter
            cols = slice(head * HD, (head + 1) * HD)
            out_ref[at, 0:Q, :] = part_k[:, cols]
            out_ref[at, Q : 2 * Q, :] = part_v[:, cols]
            out_ref[at, 2 * Q : CH, :] = tile
            copy = pltpu.make_async_copy(out_ref.at[at], out_hbm.at[at], out_sem.at[at])
            copy.start()
            sent.append(copy)
    for copy in sent:
        copy.wait()


def combine_kernel(place_ref, got_ref, cos_ref, sin_ref, out_ref):
    total = total_of(got_ref)
    square = total[2 * Q : 2 * Q + 1, :] + total[2 * Q + 1 : 2 * Q + 2, :]
    inv_row = lax.rsqrt(square / D + 1e-05)
    inv = to_column(inv_row, eye(Q))
    first = pl.multiple_of(place_ref[0] * Q, Q)
    keys = (total[:Q, :] * inv).astype(BF).astype(F32)
    keys = turn(keys, cos_ref[pl.ds(first, Q), :], sin_ref[pl.ds(first, Q), :]).astype(BF)
    values = (total[Q : 2 * Q, :] * inv).astype(BF)
    tile = two_halves(inv_row)
    for at in range(out_ref.shape[0]):
        out_ref[at, 0:Q, :] = keys
        out_ref[at, Q : 2 * Q, :] = values
        out_ref[at, 2 * Q : CH, :] = tile


def spans():
    found, first = [], 0
    for b in range(SEQ // Q):
        low = max(0, b - 2)
        found.append((low, first))
        first += (b + 1 - low) * Q
    return found, first


def attention_kernel(
    kv_ref, q_ref, cot_ref, seg_ref, cos_ref, sin_ref, gkv_ref, probs_ref, ds_ref, dk_ref, dv_ref
):
    blocks = SEQ // Q
    diag = eye(Q)
    seg_rows = [seg_ref[0:1, b * Q : (b + 1) * Q].astype(F32) for b in range(blocks)]
    seg_columns = [to_column(row, diag) for row in seg_rows]
    below = lax.broadcasted_iota(jnp.int32, (Q, Q), 0) <= lax.broadcasted_iota(
        jnp.int32, (Q, Q), 1
    )
    dk_ref[...] = jnp.zeros_like(dk_ref)
    dv_ref[...] = jnp.zeros_like(dv_ref)
    for b, (low, first) in enumerate(spans()[0]):
        rows = slice(b * Q, (b + 1) * Q)
        keys = jnp.concatenate([kv_ref[a, 0:Q, :] for a in range(low, b + 1)], axis=0)
        values = jnp.concatenate([kv_ref[a, Q : 2 * Q, :] for a in range(low, b + 1)], axis=0)
        cos, sin = cos_ref[rows, :], sin_ref[rows, :]
        q_rot = jnp.concatenate(
            [
                turn(q_ref[rows, h * HD : (h + 1) * HD].astype(F32), cos, sin).astype(BF)
                for h in range(2)
            ],
            axis=0,
        )
        cot = jnp.concatenate([cot_ref[rows, 0:HD], cot_ref[rows, HD:]], axis=0)
        allowed = [seg_columns[a] == seg_rows[b] for a in range(low, b)]
        allowed.append((seg_columns[b] == seg_rows[b]) & below)
        allowed = jnp.concatenate([jnp.where(a, 0.0, -1e30) for a in allowed], axis=0)
        allowed = jnp.concatenate([allowed, allowed], axis=1)
        scores = lax.dot_general(keys, q_rot, NT, preferred_element_type=F32) * SCALE
        scores = jnp.where(allowed < 0.0, -1e30, scores)
        top = jnp.max(scores, axis=0, keepdims=True)
        expo = jnp.exp(scores - top)
        probs = (expo * (1.0 / jnp.sum(expo, axis=0, keepdims=True))).astype(BF)
        d_probs = lax.dot_general(values, cot, NT, preferred_element_type=F32)
        prob_float = probs.astype(F32)
        delta = jnp.sum(prob_float * d_probs, axis=0, keepdims=True)
        d_scores = (prob_float * (d_probs - delta) * SCALE).astype(BF)
        span = slice(low * Q, (b + 1) * Q)
        dv_ref[span, :] += jnp.dot(probs, cot, preferred_element_type=F32)
        dk_ref[span, :] += jnp.dot(d_scores, q_rot, preferred_element_type=F32)
        kept = slice(first, first + (b + 1 - low) * Q)
        probs_ref[kept, :] = probs
        ds_ref[kept, :] = d_scores
    for b in range(blocks):
        rows = slice(b * Q, (b + 1) * Q)
        gkv_ref[b, 0:Q, :] = dk_ref[rows, :].astype(BF)
        gkv_ref[b, Q : 2 * Q, :] = dv_ref[rows, :].astype(BF)


def turned_kernel(step, place_ref, hid_ref, send_ref, keep_ref, turned_ref):
    for b in range(SEQ // Q):
        rows = slice(b * Q, (b + 1) * Q)
        turned_ref[:, rows] = hid_ref[rows, :].astype(F32).T.astype(BF)
    core = place_ref[1]
    for parity in range(2):
        for at in range(keep_ref.shape[1] // step):
            mine = pl.multiple_of((4 * at + 2 * parity + core) * step, step)
            other = pl.multiple_of((4 * at + 2 * parity + 1 - core) * step, step)
            rows = slice(at * step, (at + 1) * step)
            keep_ref[parity, rows, :] = turned_ref[pl.ds(mine, step), :]
            send_ref[parity, rows, :] = turned_ref[pl.ds(other, step), :]


def outputs_kernel(kv_ref, probs_ref, ds_ref, cos_ref, sin_ref, out_ref, gq_ref):
    for b, (low, first) in enumerate(spans()[0]):
        rows = slice(b * Q, (b + 1) * Q)
        keys = jnp.concatenate([kv_ref[a, 0:Q, :] for a in range(low, b + 1)], axis=0)
        values = jnp.concatenate([kv_ref[a, Q : 2 * Q, :] for a in range(low, b + 1)], axis=0)
        cos, sin = cos_ref[rows, :], sin_ref[rows, :]
        kept = slice(first, first + (b + 1 - low) * Q)
        attn = lax.dot_general(probs_ref[kept, :], values, TN, preferred_element_type=F32)
        d_q = lax.dot_general(ds_ref[kept, :], keys, TN, preferred_element_type=F32)
        for h in range(2):
            cols = slice(h * HD, (h + 1) * HD)
            out_ref[rows, cols] = attn[h * Q : (h + 1) * Q].astype(BF)
            gq_ref[rows, cols] = turn_back(d_q[h * Q : (h + 1) * Q], cos, sin).astype(BF)


def grad_sum_kernel(place_ref, got_ref, kv_ref, cos_ref, sin_ref, out_ref):
    total = total_of(got_ref)
    own = kv_ref[0, 0 : 2 * Q, :].astype(F32)
    both = total * own
    corr = to_row(jnp.sum(both[:Q] + both[Q:], axis=1, keepdims=True), eye(Q))
    first = pl.multiple_of(place_ref[0] * Q, Q)
    d_keys = turn_back(total[:Q, :], cos_ref[pl.ds(first, Q), :], sin_ref[pl.ds(first, Q), :])
    d_keys = d_keys.astype(BF)
    d_values = total[Q:, :].astype(BF)
    tile = two_halves(corr)
    for at in range(out_ref.shape[0]):
        out_ref[at, 0:Q, :] = d_keys
        out_ref[at, Q : 2 * Q, :] = d_values
        out_ref[at, 2 * Q : CH, :] = tile


def weight_kernel(got_ref, kv_ref, turned_ref, out_ref, grads_ref):
    blocks = SEQ // Q
    width = KVH * HD
    for b in range(blocks):
        rows = slice(b * Q, (b + 1) * Q)
        for head in range(KVH):
            at = head * blocks + b
            grads_ref[rows, head * HD : (head + 1) * HD] = got_ref[at, 0:Q, :]
            grads_ref[rows, width + head * HD : width + (head + 1) * HD] = got_ref[at, Q : 2 * Q, :]
    inv = [from_halves(kv_ref[b, 2 * Q : CH, :]) for b in range(blocks)]
    inv = jnp.concatenate(inv, axis=1)
    for parity in range(2):
        unit = (turned_ref[parity].astype(F32) * inv).astype(BF)
        product = jnp.dot(unit, grads_ref[...], preferred_element_type=F32)
        out_ref[parity] = product.astype(BF)


def hidden_kernel(got_ref, kv_ref, hid_ref, gain_ref, wk_ref, wv_ref, out_ref):
    blocks = SEQ // Q
    diag = eye(Q)
    wk, wv = wk_ref[...], wv_ref[...]
    for b in range(blocks):
        rows = slice(b * Q, (b + 1) * Q)
        mine = [got_ref[head * blocks + b] for head in range(KVH)]
        d_keys = jnp.concatenate([m[0:Q] for m in mine], axis=1)
        d_values = jnp.concatenate([m[Q : 2 * Q] for m in mine], axis=1)
        inv = to_column(from_halves(kv_ref[b, 2 * Q : CH, :]), diag)
        corr = sum(from_halves(m[2 * Q : CH]) for m in mine)
        corr = to_column(corr, diag) / D
        d_normed = lax.dot_general(d_keys, wk, NT, preferred_element_type=F32)
        d_normed += lax.dot_general(d_values, wv, NT, preferred_element_type=F32)
        unit = hid_ref[rows, :].astype(F32) * inv
        out_ref[rows, :] = (inv * (d_normed * gain_ref[...] - unit * corr)).astype(BF)


def pair_kernel(place_ref, keep_ref, got_ref, out_ref):
    at = 1 - place_ref[3]
    out_ref[...] = (keep_ref[at].astype(F32) + got_ref[at].astype(F32)).astype(BF)


def four_kernel(place_ref, keep_ref, got_ref, next_ref, out_ref):
    at = place_ref[3]
    total = keep_ref[at].astype(F32) + got_ref[at].astype(F32) + next_ref[...].astype(F32)
    out_ref[...] = total.astype(BF)


def own_rows_kernel(place_ref, gain_ref, wk_ref, wv_ref, out_ref):
    step, width = out_ref.shape[0], KVH * HD
    first = pl.multiple_of(place_ref[2] * step, step)
    lanes = lax.broadcasted_iota(jnp.int32, (step, gain_ref.shape[1]), 1)
    rows = lax.broadcasted_iota(jnp.int32, (step, gain_ref.shape[1]), 0)
    gain = jnp.sum(jnp.where(lanes == rows + first, gain_ref[...], 0.0), axis=1, keepdims=True)
    out_ref[:, 0:width] = wk_ref[pl.ds(first, step), :].astype(F32)
    out_ref[:, width : 2 * width] = wv_ref[pl.ds(first, step), :].astype(F32)
    out_ref[:, 2 * width :] = jnp.broadcast_to(gain, (step, HD))


def finish_kernel(got_ref, rows_ref, gk_ref, gv_ref, gg_ref):
    step, width = gk_ref.shape
    total = total_of(got_ref)
    gain = rows_ref[:, 2 * width : 2 * width + 1]
    gk_ref[...] = total[:, :width] * gain
    gv_ref[...] = total[:, width:] * gain
    along = rows_ref[:, 0 : 2 * width] * total
    gg_ref[...] = to_row(jnp.sum(along, axis=1, keepdims=True), eye(step))


VMEM = pl.BlockSpec(memory_space=pltpu.VMEM)
SMEM = pl.BlockSpec(memory_space=pltpu.SMEM)
HBM = pl.BlockSpec(memory_space=pltpu.HBM)


def call(kernel, name, out_shape, in_specs, out_specs=None, scratch=(), cost=None, grant=16):
    many = isinstance(out_shape, (list, tuple))
    if out_specs is None:
        out_specs = [VMEM] * len(out_shape) if many else VMEM
    flops, size = cost
    return pl.pallas_call(
        kernel,
        out_shape=out_shape,
        in_specs=in_specs,
        out_specs=out_specs,
        scratch_shapes=list(scratch),
        compiler_params=pltpu.CompilerParams(vmem_limit_bytes=grant * 1024 * 1024),
        cost_estimate=pl.CostEstimate(flops=int(flops), bytes_accessed=int(size), transcendentals=0),
        name=name,
    )


def body(nz, hidden_in, norm_gain, key_weight, value_weight, queries, segments, cotangent):
    shape = jax.ShapeDtypeStruct
    width = KVH * HD
    feats = hidden_in.shape[1]
    step = feats // (2 * nz)
    quarter = feats // 4
    blocks = SEQ // Q
    kept = spans()[1]
    dma = pltpu.SemaphoreType.DMA
    cos, sin = (jnp.asarray(t) for t in rope_tables())
    gain = norm_gain.reshape(1, feats)
    core, parity = lax.axis_index("core"), lax.axis_index("zl")
    at = (lax.axis_index("zh") * 2 + parity) * 2 + core
    place = jnp.stack([lax.axis_index("y"), core, at, parity]).astype(jnp.int32)

    parts = call(
        project_kernel,
        "project",
        shape((KVH * blocks, CH, HD), BF),
        [HBM] * 4,
        HBM,
        [
            pltpu.VMEM((SEQ, feats), BF),
            pltpu.VMEM((1, feats), F32),
            pltpu.VMEM((feats, width), BF),
            pltpu.VMEM((feats, width), BF),
            pltpu.VMEM((KVH * blocks, CH, HD), BF),
            dma((13,)),
            dma((KVH * blocks,)),
        ],
        cost=(4 * SEQ * feats * width, 2.5e6),
        grant=60,
    )(hidden_in, gain, key_weight, value_weight)
    parts, hidden, place = lax.optimization_barrier((parts, hidden_in, place))
    turned_send, turned_keep = call(
        functools.partial(turned_kernel, step),
        "turned",
        [shape((2, quarter, SEQ), BF)] * 2,
        [SMEM, VMEM],
        scratch=[pltpu.VMEM((feats, SEQ), BF)],
        cost=(SEQ * feats, 1.5e6),
    )(place, hidden)
    own_rows = call(
        own_rows_kernel,
        "own_rows",
        shape((step, 2 * width + HD), F32),
        [SMEM] + [VMEM] * 3,
        cost=(SEQ * feats, 1e6),
    )(place, gain, key_weight, value_weight)
    parts = lax.all_to_all(parts, ("x", "y"), 0, 0, tiled=True)
    parts, turned_send, turned_keep, own_rows = lax.optimization_barrier(
        (parts, turned_send, turned_keep, own_rows)
    )
    own = call(
        combine_kernel,
        "combine",
        shape((blocks, CH, HD), BF),
        [SMEM] + [VMEM] * 3,
        cost=(16 * CH * HD, 1.5e6),
    )(place, parts, cos, sin)
    kv = lax.all_to_all(own, "y", 0, 0, tiled=True)
    grad_parts, probs, d_scores = call(
        attention_kernel,
        "attention",
        [shape((blocks, 2 * Q, HD), BF), shape((kept, 2 * Q), BF), shape((kept, 2 * Q), BF)],
        [VMEM] * 6,
        scratch=[pltpu.VMEM((SEQ, HD), F32), pltpu.VMEM((SEQ, HD), F32)],
        cost=(8 * kept * 2 * Q * HD, 2e6),
    )(kv, queries, cotangent, segments, cos, sin)
    grad_parts = lax.all_to_all(grad_parts, "y", 0, 0, tiled=True)
    grad_own = call(
        grad_sum_kernel,
        "grad_sum",
        shape((KVH * blocks, CH, HD), BF),
        [SMEM] + [VMEM] * 4,
        cost=(16 * CH * HD, 1.5e6),
    )(place, grad_parts, own, cos, sin)
    grads = lax.all_to_all(grad_own, ("x", "y"), 0, 0, tiled=True)

    def product(turned, name):
        return call(
            weight_kernel,
            name,
            shape((2, quarter, 2 * width), BF),
            [VMEM] * 3,
            scratch=[pltpu.VMEM((SEQ, 2 * width), BF)],
            cost=(4 * SEQ * feats // 2 * width, 2e6),
        )(grads, kv, turned)

    swap = [(0, 1), (1, 0)]
    send = product(turned_send, "weight_send")
    send, turned_keep = lax.optimization_barrier((send, turned_keep))
    got = lax.ppermute(send, "core", swap)
    keep = product(turned_keep, "weight_keep")
    pair = call(
        pair_kernel,
        "pair",
        shape((quarter, 2 * width), BF),
        [SMEM] + [VMEM] * 2,
        cost=(quarter * 2 * width, 1e6),
    )(place, keep, got)
    pair, probs, grads = lax.optimization_barrier((pair, probs, grads))
    got_pair = lax.ppermute(pair, "zl", swap)
    grad_hidden = call(
        hidden_kernel,
        "hidden",
        shape(hidden_in.shape, BF),
        [VMEM] * 6,
        cost=(4 * SEQ * feats * width, 4e6),
    )(grads, kv, hidden_in, gain, key_weight, value_weight)
    attn_out, grad_queries = call(
        outputs_kernel,
        "outputs",
        [shape(queries.shape, BF), shape(queries.shape, BF)],
        [VMEM] * 5,
        cost=(4 * kept * 2 * Q * HD, 2e6),
    )(kv, probs, d_scores, cos, sin)
    got_pair, grad_hidden, attn_out, grad_queries = lax.optimization_barrier(
        (got_pair, grad_hidden, attn_out, grad_queries)
    )
    four = call(
        four_kernel,
        "four",
        shape((quarter, 2 * width), BF),
        [SMEM] + [VMEM] * 3,
        cost=(quarter * 2 * width, 1e6),
    )(place, keep, got, got_pair)
    rows = lax.all_to_all(four.reshape(nz // 2, step, 2 * width), "zh", 0, 0, tiled=True)
    grad_key, grad_value, grad_gain = call(
        finish_kernel,
        "finish",
        [shape((step, width), F32), shape((step, width), F32), shape((1, step), F32)],
        [VMEM] * 2,
        cost=(quarter * 2 * width, 1e6),
    )(rows, own_rows)
    return (attn_out, grad_hidden, grad_queries, grad_key, grad_value, grad_gain.reshape(step))


def solution(mesh):
    nz = mesh.devices.shape[0] // 2
    split = Mesh(mesh.devices.reshape(nz // 2, 2, 2, 4, 4), ("zh", "zl", "core", "x", "y"))
    dp, tensor = ("zh", "zl", "core"), ("x", "y")
    return jax.shard_map(
        functools.partial(body, nz),
        mesh=split,
        in_specs=(
            P(dp, tensor),
            P(tensor),
            P(tensor, None),
            P(tensor, None),
            P(dp, tensor),
            P(dp, None),
            P(dp, tensor),
        ),
        out_specs=(
            P(dp, tensor),
            P(dp, tensor),
            P(dp, tensor),
            P(tensor + dp, None),
            P(tensor + dp, None),
            P(tensor + dp),
        ),
        check_vma=False,
    )
```

```python
import functools

import jax
import jax.numpy as jnp
import numpy as np
from jax import lax
from jax.experimental import pallas as pl
from jax.experimental.pallas import tpu as pltpu
from jax.sharding import Mesh, PartitionSpec as P

D = 8192
SEQ = 512
KVH = 4
HD = 128
SCALE = 1.0 / HD**0.5
ROPE_BASE = 500000.0
Q = 128
CH = 2 * Q + 16
NT = (((1,), (1,)), ((), ()))
TN = (((0,), (0,)), ((), ()))
BF = jnp.bfloat16
F32 = jnp.float32


def rope_tables():
    half = HD // 2
    freq = np.float32(ROPE_BASE) ** (-(np.arange(half, dtype=np.float32) * np.float32(2.0 / HD)))
    angle = (np.arange(SEQ, dtype=np.float32)[:, None] * freq[None, :]).astype(np.float64)
    cos, sin = np.cos(angle), np.sin(angle)
    return (
        np.concatenate([cos, cos], axis=1).astype(np.float32),
        np.concatenate([-sin, sin], axis=1).astype(np.float32),
    )


def eye(n):
    return lax.broadcasted_iota(jnp.int32, (n, n), 0) == lax.broadcasted_iota(jnp.int32, (n, n), 1)


def to_column(row, diag):
    return jnp.sum(jnp.where(diag, row, 0.0), axis=1, keepdims=True)


def to_row(column, diag):
    return jnp.sum(jnp.where(diag, column, 0.0), axis=0, keepdims=True)


def two_halves(row):
    lead = row.astype(BF)
    rest = (row - lead.astype(F32)).astype(BF)
    at = lax.broadcasted_iota(jnp.int32, (16, HD), 0)
    zero = jnp.zeros((), F32)
    both = jnp.where(at == 0, lead.astype(F32), jnp.where(at == 1, rest.astype(F32), zero))
    return both.astype(BF)


def from_halves(tile):
    both = tile.astype(F32)
    return both[0:1, :] + both[1:2, :]


def turn(vec, cos, sin):
    return vec * cos + pltpu.roll(vec, HD // 2, 1) * sin


def turn_back(vec, cos, sin):
    return vec * cos - pltpu.roll(vec, HD // 2, 1) * sin


def total_of(got_ref):
    total = got_ref[0].astype(F32)
    for at in range(1, got_ref.shape[0]):
        total += got_ref[at].astype(F32)
    return total


def project_kernel(
    step, hid_hbm, gain_hbm, wk_hbm, wv_hbm, q_hbm, seg_hbm, cos_hbm, sin_hbm,
    out_ref, send_ref, keep_ref, q_rot_ref, bias_ref, angle_ref,
    hid_ref, gain_ref, wk_ref, wv_ref, q_ref, seg_ref, cos_ref, sin_ref, scaled_ref, turned_ref, sem
):
    quarters = SEQ // Q
    feats = hid_ref.shape[1]
    gain_copy = pltpu.make_async_copy(gain_hbm, gain_ref, sem.at[0])
    hid_copies = []
    for at in range(quarters):
        rows = pl.ds(at * Q, Q)
        hid_copies.append(pltpu.make_async_copy(hid_hbm.at[rows, :], hid_ref.at[rows, :], sem.at[1 + at]))
    weight_copies = [
        pltpu.make_async_copy(wk_hbm, wk_ref, sem.at[5]),
        pltpu.make_async_copy(wv_hbm, wv_ref, sem.at[6]),
    ]
    late_copies = [
        pltpu.make_async_copy(src, dst, sem.at[7 + at])
        for at, (src, dst) in enumerate(
            ((q_hbm, q_ref), (seg_hbm, seg_ref), (cos_hbm, cos_ref), (sin_hbm, sin_ref))
        )
    ]
    for copy in [gain_copy] + hid_copies + weight_copies + late_copies:
        copy.start()
    ones = jnp.ones((16, HD), BF)
    gain_copy.wait()
    for quarter in range(quarters):
        hid_copies[quarter].wait()
        rows = slice(quarter * Q, (quarter + 1) * Q)
        hid = hid_ref[rows, :].astype(F32)
        scaled_ref[rows, :] = (hid * gain_ref[...]).astype(BF)
        turned_ref[:, rows] = hid.T.astype(BF)
        square = hid * hid
        square = sum(square[:, c * HD : (c + 1) * HD] for c in range(feats // HD))
        lead = square.astype(BF)
        rest = (square - lead.astype(F32)).astype(BF)
        sums = lax.dot_general(ones, lead, NT, preferred_element_type=F32)
        sums += lax.dot_general(ones, rest, NT, preferred_element_type=F32)
        tile = two_halves(sums[0:1, :])
        for head in range(KVH):
            out_ref[head * quarters + quarter, 2 * Q : CH, :] = tile
    for which, weight_ref in enumerate((wk_ref, wv_ref)):
        weight_copies[which].wait()
        part = jnp.dot(scaled_ref[...], weight_ref[...], preferred_element_type=F32).astype(BF)
        for quarter in range(quarters):
            for head in range(KVH):
                out_ref[head * quarters + quarter, which * Q : (which + 1) * Q, :] = part[
                    quarter * Q : (quarter + 1) * Q, head * HD : (head + 1) * HD
                ]
    core = lax.axis_index("core")
    for which in range(2):
        parity = lax.axis_index("zl") if which == 0 else 1 - lax.axis_index("zl")
        for at in range(keep_ref.shape[1] // step):
            mine = pl.multiple_of((4 * at + 2 * parity + core) * step, step)
            other = pl.multiple_of((4 * at + 2 * parity + 1 - core) * step, step)
            rows = slice(at * step, (at + 1) * step)
            keep_ref[which, rows, :] = turned_ref[pl.ds(mine, step), :]
            send_ref[which, rows, :] = turned_ref[pl.ds(other, step), :]
    for copy in late_copies:
        copy.wait()
    own = pl.ds(pl.multiple_of(lax.axis_index("y") * Q, Q), Q)
    angle_ref[0] = cos_ref[own, :]
    angle_ref[1] = sin_ref[own, :]
    diag = eye(Q)
    below = lax.broadcasted_iota(jnp.int32, (Q, Q), 0) <= lax.broadcasted_iota(
        jnp.int32, (Q, Q), 1
    )
    seg_rows = [seg_ref[0:1, b * Q : (b + 1) * Q].astype(F32) for b in range(quarters)]
    seg_columns = [to_column(row, diag) for row in seg_rows]
    for b, (low, first) in enumerate(spans()[0]):
        rows = slice(b * Q, (b + 1) * Q)
        cos, sin = cos_ref[rows, :], sin_ref[rows, :]
        for h in range(2):
            turned = turn(q_ref[rows, h * HD : (h + 1) * HD].astype(F32), cos, sin)
            q_rot_ref[b, h * Q : (h + 1) * Q, :] = turned.astype(BF)
        for a in range(low, b + 1):
            same = seg_columns[a] == seg_rows[b]
            allowed = same & below if a == b else same
            at = first + (a - low) * Q
            bias_ref[at : at + Q, :] = jnp.where(allowed, 0.0, -1e30)


def combine_kernel(got_ref, angle_ref, out_ref):
    total = total_of(got_ref)
    square = total[2 * Q : 2 * Q + 1, :] + total[2 * Q + 1 : 2 * Q + 2, :]
    inv_row = lax.rsqrt(square / D + 1e-05)
    inv = to_column(inv_row, eye(Q))
    keys = (total[:Q, :] * inv).astype(BF).astype(F32)
    keys = turn(keys, angle_ref[0], angle_ref[1]).astype(BF)
    values = (total[Q : 2 * Q, :] * inv).astype(BF)
    tile = two_halves(inv_row)
    for at in range(out_ref.shape[0]):
        out_ref[at, 0:Q, :] = keys
        out_ref[at, Q : 2 * Q, :] = values
        out_ref[at, 2 * Q : CH, :] = tile


def spans():
    found, first = [], 0
    for b in range(SEQ // Q):
        low = max(0, b - 2)
        found.append((low, first))
        first += (b + 1 - low) * Q
    return found, first


def attention_kernel(kv_ref, q_rot_ref, cot_ref, bias_ref, gkv_ref, probs_ref, ds_ref):
    blocks = SEQ // Q
    cots = []
    for b, (low, first) in enumerate(spans()[0]):
        rows = slice(b * Q, (b + 1) * Q)
        keys = jnp.concatenate([kv_ref[a, 0:Q, :] for a in range(low, b + 1)], axis=0)
        values = jnp.concatenate([kv_ref[a, Q : 2 * Q, :] for a in range(low, b + 1)], axis=0)
        q_rot = q_rot_ref[b]
        cot = jnp.concatenate([cot_ref[rows, 0:HD], cot_ref[rows, HD:]], axis=0)
        cots.append(cot)
        kept = slice(first, first + (b + 1 - low) * Q)
        bias = jnp.concatenate([bias_ref[kept, :]] * 2, axis=1)
        scores = lax.dot_general(keys, q_rot, NT, preferred_element_type=F32) + bias
        top = jnp.max(scores, axis=0, keepdims=True)
        expo = jnp.exp((scores - top) * SCALE)
        probs = (expo * (1.0 / jnp.sum(expo, axis=0, keepdims=True))).astype(BF)
        d_probs = lax.dot_general(values, cot, NT, preferred_element_type=F32)
        prob_float = probs.astype(F32)
        delta = jnp.sum(prob_float * d_probs, axis=0, keepdims=True)
        probs_ref[kept, :] = probs
        ds_ref[kept, :] = (prob_float * (d_probs - delta)).astype(BF)
    for a in range(blocks):
        wide, deep, queries, cotangents = [], [], [], []
        for b, (low, first) in enumerate(spans()[0]):
            if low <= a <= b:
                at = first + (a - low) * Q
                wide.append(probs_ref[at : at + Q, :])
                deep.append(ds_ref[at : at + Q, :])
                queries.append(q_rot_ref[b])
                cotangents.append(cots[b])
        wide, deep = jnp.concatenate(wide, axis=1), jnp.concatenate(deep, axis=1)
        queries, cotangents = jnp.concatenate(queries, axis=0), jnp.concatenate(cotangents, axis=0)
        d_values = jnp.dot(wide, cotangents, preferred_element_type=F32)
        d_keys = jnp.dot(deep, queries, preferred_element_type=F32)
        gkv_ref[a, 0:Q, :] = (d_keys * SCALE).astype(BF)
        gkv_ref[a, Q : 2 * Q, :] = d_values.astype(BF)


def outputs_kernel(kv_ref, probs_ref, ds_ref, cos_ref, sin_ref, out_ref, gq_ref):
    for b, (low, first) in enumerate(spans()[0]):
        rows = slice(b * Q, (b + 1) * Q)
        keys = jnp.concatenate([kv_ref[a, 0:Q, :] for a in range(low, b + 1)], axis=0)
        values = jnp.concatenate([kv_ref[a, Q : 2 * Q, :] for a in range(low, b + 1)], axis=0)
        cos, sin = cos_ref[rows, :], sin_ref[rows, :]
        kept = slice(first, first + (b + 1 - low) * Q)
        attn = lax.dot_general(probs_ref[kept, :], values, TN, preferred_element_type=F32)
        d_q = lax.dot_general(ds_ref[kept, :], keys, TN, preferred_element_type=F32)
        for h in range(2):
            cols = slice(h * HD, (h + 1) * HD)
            out_ref[rows, cols] = attn[h * Q : (h + 1) * Q].astype(BF)
            d_query = d_q[h * Q : (h + 1) * Q] * SCALE
            gq_ref[rows, cols] = turn_back(d_query, cos, sin).astype(BF)


def grad_sum_kernel(got_ref, kv_ref, angle_ref, out_ref):
    total = total_of(got_ref)
    own = kv_ref[0, 0 : 2 * Q, :].astype(F32)
    both = total * own
    corr = to_row(jnp.sum(both[:Q] + both[Q:], axis=1, keepdims=True), eye(Q))
    d_keys = turn_back(total[:Q, :], angle_ref[0], angle_ref[1])
    inv = to_column(from_halves(kv_ref[0, 2 * Q : CH, :]), eye(Q))
    d_keys = (d_keys * inv).astype(BF)
    d_values = (total[Q:, :] * inv).astype(BF)
    tile = two_halves(corr)
    for at in range(out_ref.shape[0]):
        out_ref[at, 0:Q, :] = d_keys
        out_ref[at, Q : 2 * Q, :] = d_values
        out_ref[at, 2 * Q : CH, :] = tile


def weight_kernel(got_ref, turned_ref, out_ref):
    blocks = SEQ // Q
    width = KVH * HD
    for which in range(2):
        for pair in range(KVH // 2):
            columns = []
            for head in (2 * pair, 2 * pair + 1):
                part = [
                    got_ref[head * blocks + b, which * Q : (which + 1) * Q, :] for b in range(blocks)
                ]
                columns.append(jnp.concatenate(part, axis=0))
            grads = jnp.concatenate(columns, axis=1)
            at = which * width + 2 * pair * HD
            for parity in range(2):
                product = jnp.dot(turned_ref[parity], grads, preferred_element_type=F32)
                out_ref[parity, :, at : at + 2 * HD] = product.astype(BF)


def hidden_kernel(got_ref, kv_ref, hid_ref, gain_ref, wk_ref, wv_ref, out_ref):
    blocks = SEQ // Q
    diag = eye(Q)
    wk, wv = wk_ref[...], wv_ref[...]
    for b in range(blocks):
        rows = slice(b * Q, (b + 1) * Q)
        mine = [got_ref[head * blocks + b] for head in range(KVH)]
        d_keys = jnp.concatenate([m[0:Q] for m in mine], axis=1)
        d_values = jnp.concatenate([m[Q : 2 * Q] for m in mine], axis=1)
        inv = to_column(from_halves(kv_ref[b, 2 * Q : CH, :]), diag)
        corr = sum(from_halves(m[2 * Q : CH]) for m in mine)
        corr = to_column(corr, diag) / D
        d_normed = lax.dot_general(d_keys, wk, NT, preferred_element_type=F32)
        d_normed += lax.dot_general(d_values, wv, NT, preferred_element_type=F32)
        hid = hid_ref[rows, :].astype(F32)
        out_ref[rows, :] = (d_normed * gain_ref[...] - hid * (inv * inv * corr)).astype(BF)


def pair_kernel(keep_ref, got_ref, out_ref):
    out_ref[...] = (keep_ref[1].astype(F32) + got_ref[1].astype(F32)).astype(BF)


def four_kernel(keep_ref, got_ref, next_ref, out_ref):
    total = keep_ref[0].astype(F32) + got_ref[0].astype(F32) + next_ref[...].astype(F32)
    out_ref[...] = total.astype(BF)


def own_rows_kernel(gain_ref, wk_ref, wv_ref, out_ref):
    step, width = out_ref.shape[0], KVH * HD
    place = (lax.axis_index("zh") * 2 + lax.axis_index("zl")) * 2 + lax.axis_index("core")
    first = pl.multiple_of(place * step, step)
    lanes = lax.broadcasted_iota(jnp.int32, (step, gain_ref.shape[1]), 1)
    rows = lax.broadcasted_iota(jnp.int32, (step, gain_ref.shape[1]), 0)
    gain = jnp.sum(jnp.where(lanes == rows + first, gain_ref[...], 0.0), axis=1, keepdims=True)
    out_ref[:, 0:width] = wk_ref[pl.ds(first, step), :].astype(F32)
    out_ref[:, width : 2 * width] = wv_ref[pl.ds(first, step), :].astype(F32)
    out_ref[:, 2 * width :] = jnp.broadcast_to(gain, (step, HD))


def finish_kernel(got_ref, rows_ref, gk_ref, gv_ref, gg_ref):
    step, width = gk_ref.shape
    total = total_of(got_ref)
    gain = rows_ref[:, 2 * width : 2 * width + 1]
    gk_ref[...] = total[:, :width] * gain
    gv_ref[...] = total[:, width:] * gain
    along = rows_ref[:, 0 : 2 * width] * total
    gg_ref[...] = to_row(jnp.sum(along, axis=1, keepdims=True), eye(step))


def neighbours(nz):
    pairs = []
    for z in range(nz):
        for core in range(2):
            other = (z ^ 1) if core == 0 else ((z + nz - 1) % nz if z % 2 == 0 else (z + 1) % nz)
            pairs.append((2 * z + core, 2 * other + core))
    return pairs


def in_hbm(array):
    return pltpu.with_memory_space_constraint(array, pltpu.HBM)


VMEM = pl.BlockSpec(memory_space=pltpu.VMEM)
HBM = pl.BlockSpec(memory_space=pltpu.HBM)


def call(kernel, name, out_shape, in_specs, out_specs=None, scratch=(), cost=None, grant=16):
    many = isinstance(out_shape, (list, tuple))
    if out_specs is None:
        out_specs = [VMEM] * len(out_shape) if many else VMEM
    flops, size = cost
    return pl.pallas_call(
        kernel,
        out_shape=out_shape,
        in_specs=in_specs,
        out_specs=out_specs,
        scratch_shapes=list(scratch),
        compiler_params=pltpu.CompilerParams(vmem_limit_bytes=grant * 1024 * 1024),
        cost_estimate=pl.CostEstimate(flops=int(flops), bytes_accessed=int(size), transcendentals=0),
        name=name,
    )


def body(nz, hidden_in, norm_gain, key_weight, value_weight, queries, segments, cotangent):
    shape = jax.ShapeDtypeStruct
    width = KVH * HD
    feats = hidden_in.shape[1]
    step = feats // (2 * nz)
    quarter = feats // 4
    blocks = SEQ // Q
    kept = spans()[1]
    dma = pltpu.SemaphoreType.DMA
    cos, sin = (jnp.asarray(t) for t in rope_tables())
    gain = norm_gain.reshape(1, feats)

    parts, turned_send, turned_keep, q_rot, bias, angle = call(
        functools.partial(project_kernel, step),
        "project",
        [
            shape((KVH * blocks, CH, HD), BF),
            shape((2, quarter, SEQ), BF),
            shape((2, quarter, SEQ), BF),
            shape((blocks, 2 * Q, HD), BF),
            shape((kept, Q), F32),
            shape((2, Q, HD), F32),
        ],
        [HBM] * 8,
        scratch=[
            pltpu.VMEM((SEQ, feats), BF),
            pltpu.VMEM((1, feats), F32),
            pltpu.VMEM((feats, width), BF),
            pltpu.VMEM((feats, width), BF),
            pltpu.VMEM(queries.shape, BF),
            pltpu.VMEM(segments.shape, jnp.int32),
            pltpu.VMEM((SEQ, HD), F32),
            pltpu.VMEM((SEQ, HD), F32),
            pltpu.VMEM((SEQ, feats), BF),
            pltpu.VMEM((feats, SEQ), BF),
            dma((11,)),
        ],
        cost=(4 * SEQ * feats * width, 4e6),
    )(*(in_hbm(a) for a in (hidden_in, gain, key_weight, value_weight, queries, segments, cos, sin)))
    parts = lax.all_to_all(parts, ("x", "y"), 0, 0, tiled=True)
    own = call(
        combine_kernel,
        "combine",
        shape((blocks, CH, HD), BF),
        [VMEM] * 2,
        cost=(16 * CH * HD, 1.5e6),
    )(parts, angle)
    kv = lax.all_to_all(own, "y", 0, 0, tiled=True)
    grad_parts, probs, d_scores = call(
        attention_kernel,
        "attention",
        [shape((blocks, 2 * Q, HD), BF), shape((kept, 2 * Q), BF), shape((kept, 2 * Q), BF)],
        [VMEM] * 4,
        cost=(8 * kept * 2 * Q * HD, 2e6),
    )(kv, q_rot, cotangent, bias)
    grad_parts = lax.all_to_all(grad_parts, "y", 0, 0, tiled=True)
    grad_own = call(
        grad_sum_kernel,
        "grad_sum",
        shape((KVH * blocks, CH, HD), BF),
        [VMEM] * 3,
        cost=(16 * CH * HD, 1.5e6),
    )(grad_parts, own, angle)
    grads = lax.all_to_all(grad_own, ("x", "y"), 0, 0, tiled=True)

    def product(turned, name):
        return call(
            weight_kernel,
            name,
            shape((2, quarter, 2 * width), BF),
            [VMEM] * 2,
            cost=(4 * SEQ * feats // 2 * width, 2e6),
        )(grads, turned)

    swap = [(0, 1), (1, 0)]
    send = product(turned_send, "weight_send")
    send, turned_keep = lax.optimization_barrier((send, turned_keep))
    got = lax.ppermute(send, "core", swap)
    keep = product(turned_keep, "weight_keep")
    pair = call(
        pair_kernel,
        "pair",
        shape((quarter, 2 * width), BF),
        [VMEM] * 2,
        cost=(quarter * 2 * width, 1e6),
    )(keep, got)
    pair, probs, grads, gain_late = lax.optimization_barrier((pair, probs, grads, gain))
    got_pair = lax.ppermute(pair, ("zh", "zl", "core"), neighbours(nz))
    own_rows = call(
        own_rows_kernel,
        "own_rows",
        shape((step, 2 * width + HD), F32),
        [VMEM] * 3,
        cost=(SEQ * feats, 1e6),
    )(gain_late, key_weight, value_weight)
    grad_hidden = call(
        hidden_kernel,
        "hidden",
        shape(hidden_in.shape, BF),
        [VMEM] * 6,
        cost=(4 * SEQ * feats * width, 4e6),
    )(grads, kv, hidden_in, gain, key_weight, value_weight)
    attn_out, grad_queries = call(
        outputs_kernel,
        "outputs",
        [shape(queries.shape, BF), shape(queries.shape, BF)],
        [VMEM] * 5,
        cost=(4 * kept * 2 * Q * HD, 2e6),
    )(kv, probs, d_scores, cos, sin)
    got_pair, grad_hidden, attn_out, grad_queries, own_rows = lax.optimization_barrier(
        (got_pair, grad_hidden, attn_out, grad_queries, own_rows)
    )
    four = call(
        four_kernel,
        "four",
        shape((quarter, 2 * width), BF),
        [VMEM] * 3,
        cost=(quarter * 2 * width, 1e6),
    )(keep, got, got_pair)
    rows = lax.all_to_all(four.reshape(nz // 2, step, 2 * width), "zh", 0, 0, tiled=True)
    grad_key, grad_value, grad_gain = call(
        finish_kernel,
        "finish",
        [shape((step, width), F32), shape((step, width), F32), shape((1, step), F32)],
        [VMEM] * 2,
        cost=(quarter * 2 * width, 1e6),
    )(rows, own_rows)
    return (attn_out, grad_hidden, grad_queries, grad_key, grad_value, grad_gain.reshape(step))


def solution(mesh):
    nz = mesh.devices.shape[0] // 2
    split = Mesh(mesh.devices.reshape(nz // 2, 2, 2, 4, 4), ("zh", "zl", "core", "x", "y"))
    dp, tensor = ("zh", "zl", "core"), ("x", "y")
    return jax.shard_map(
        functools.partial(body, nz),
        mesh=split,
        in_specs=(
            P(dp, tensor),
            P(tensor),
            P(tensor, None),
            P(tensor, None),
            P(dp, tensor),
            P(dp, None),
            P(dp, tensor),
        ),
        out_specs=(
            P(dp, tensor),
            P(dp, tensor),
            P(dp, tensor),
            P(tensor + dp, None),
            P(tensor + dp, None),
            P(tensor + dp),
        ),
        check_vma=False,
    )
```
